32 devices in a mesh: mem: 8 (over z, y), dom: 4 (over x, core).
Axes of the slice: x: 2, y: 2, z: 4, core: 2. Of those that a mesh axis runs over, the one named last changes fastest.
Arguments:
- fcst_pert: float32 [2, 1024, 4, 1024], P(None, 'mem', 'dom'), may hold values from -6 to 6
- sensitivity: float32 [2, 64, 4, 1024], P(None, None, 'dom', 'mem'), may hold values from -6 to 6
- obs_pert: float32 [24576, 1024], P(('mem', 'dom')), may hold values from -6 to 6
- weighted_innovation: float32 [24576], P(('mem', 'dom')), may hold values from -8 to 8
- obs_lists: int32 [8, 16], replicated, may hold values from 0 to 191, as said below
- block_taper: float32 [8, 16], replicated, may hold values from 0.2 to 1
- counts: int32 [8], replicated, may hold values from 8 to 16, as said below
Outputs:
- impact: float32 [24576, 128], P(('mem', 'dom'))
The draws below stay inside these ranges and needn't reach their ends.
Inputs may be any that keep to these rules, and one draw needn't show every extreme that they name: `obs_lists`: each row's ids are distinct, and every id names an observation block whose column block is within one of the row's column block, cyclically. Observation block o belongs to column block o // 24 and region (o // 6) % 4. The first 8 slots of each row name, for every region, one block of the column block before and one of the column block after. `counts`: some column block uses all 16 slots.
All inputs are finite; a program needn't handle non-finite values.
Results may differ from the reference program's by a relative error of at most 0.0003.
Values sent between devices are 32-bit elements; how exact they have to be, the bound alone decides.
A program may use at most 128 MiB of HBM per device.

```python
import jax
import jax.numpy as jnp
from jax import lax

M = 1024
T_SIZE = 64
LEADS = 2
OBSB = 128
LMAX = 16
BLK_DEV = 6
COL_DEV = 128
REGIONS = 4
CBLK = 8
LEV = 4
COLS = 1024
OBLK = 192
OBS = 24576


def draw_obs_lists(key, part):
    candidates = 3 * REGIONS * BLK_DEV
    list_key = jax.random.fold_in(key, 11)
    inner_key, order_key = jax.random.split(list_key)
    chosen_inner = jax.random.randint(inner_key, (CBLK, 3, REGIONS), 0, BLK_DEV, dtype=jnp.int32)
    cand = jnp.arange(candidates, dtype=jnp.int32)
    cand_offset = cand // (REGIONS * BLK_DEV)
    cand_region = cand // BLK_DEV % REGIONS
    cand_inner = cand % BLK_DEV
    picked_inner = chosen_inner[:, cand_offset, cand_region]
    forced = (cand_offset[None, :] != 1) & (cand_inner[None, :] == picked_inner)
    row_keys = jax.random.split(order_key, CBLK)
    perms = jax.vmap(lambda one_key: jax.random.permutation(one_key, candidates))(row_keys).astype(jnp.int32)
    scores = jnp.where(forced, perms, perms + candidates)
    order = jnp.argsort(scores, axis=1, stable=True).astype(jnp.int32)
    picks = order[:, :LMAX]
    offsets = picks // (REGIONS * BLK_DEV) - 1
    region_ids = picks // BLK_DEV % REGIONS
    inner_ids = picks % BLK_DEV
    column_ids = (jnp.arange(CBLK, dtype=jnp.int32)[:, None] + offsets) % CBLK
    return ((column_ids * REGIONS + region_ids) * BLK_DEV + inner_ids).astype(jnp.int32)


def draw_counts(key, part):
    count_key, place_key = jax.random.split(jax.random.fold_in(key, 23))
    drawn = jax.random.randint(count_key, (CBLK,), 2 * REGIONS, LMAX + 1, dtype=jnp.int32)
    fullest = jax.random.randint(place_key, (), 0, CBLK, dtype=jnp.int32)
    return drawn.at[fullest].set(LMAX).astype(jnp.int32)


def block_levels(stream_key, dims, cuts, low, largest):
    gain, own = 1.0, jax.random.fold_in(stream_key, 6)
    for position, blocks in cuts:
        steps = jnp.exp(jax.random.uniform(jax.random.fold_in(own, position), (blocks,), jnp.float32, low / len(cuts), largest / len(cuts)))
        gain = gain * jnp.repeat(steps, dims[position] // blocks).reshape([-1 if axis == position else 1 for axis in range(len(dims))])
    return gain


def gaussian(rng, dims, width, reach, shards=(), kind=jnp.bfloat16):
    values = width * jax.random.normal(rng, dims, jnp.float32)
    if shards:
        values = values * block_levels(rng, dims, shards, -0.22, 0.18)
    return jnp.clip(values, -reach, reach).astype(kind)


def setup_inputs(seed: int = 0) -> dict:
    key_list = jax.random.split(jax.random.key(seed), 8)
    fcst_pert = gaussian(key_list[0], (LEADS, M, LEV, COLS), 1.0, 6.0, ((1, 8), (2, 4)), jnp.float32)
    sensitivity = gaussian(key_list[1], (LEADS, T_SIZE, LEV, COLS), 1.0, 6.0, ((2, 4), (3, 8)), jnp.float32)
    obs_pert = gaussian(key_list[2], (OBS, M), 1.0, 6.0, ((0, 32),), jnp.float32)
    weighted_innovation = gaussian(key_list[3], (OBS,), 1.5, 8.0, ((0, 32),), jnp.float32)
    obs_lists = draw_obs_lists(jax.random.fold_in(key_list[7], 71), 0)
    block_taper = jnp.clip(jax.random.uniform(key_list[5], (CBLK, LMAX), jnp.float32, 0.2, 1.0), 0.2, 1.0)
    counts = draw_counts(jax.random.fold_in(key_list[7], 71), 0)
    return {"fcst_pert": fcst_pert, "sensitivity": sensitivity, "obs_pert": obs_pert, "weighted_innovation": weighted_innovation, "obs_lists": obs_lists, "block_taper": block_taper, "counts": counts}


def reference(fcst_pert, sensitivity, obs_pert, weighted_innovation, obs_lists, block_taper, counts):
    grid_x = fcst_pert.reshape(LEADS, M, LEV, CBLK, COL_DEV)
    grid_s = sensitivity.reshape(LEADS, T_SIZE, LEV, CBLK, COL_DEV)

    def column_sums(index):
        xpart = lax.dynamic_index_in_dim(grid_x, index, 3, keepdims=False)
        spart = lax.dynamic_index_in_dim(grid_s, index, 3, keepdims=False)
        summed = jnp.einsum('lkvc,ltvc->klt', xpart, spart, precision=lax.Precision.HIGHEST)
        return summed.reshape(M, LEADS * T_SIZE)

    contracted = lax.map(column_sums, jnp.arange(CBLK, dtype=jnp.int32))
    slot_live = jnp.arange(LMAX, dtype=jnp.int32)[None, :] < counts[:, None]
    matches = (obs_lists[:, :, None] == jnp.arange(OBLK, dtype=jnp.int32)[None, None, :]) & slot_live[:, :, None]
    weights = jnp.sum(jnp.where(matches, block_taper[:, :, None], jnp.zeros((), block_taper.dtype)), axis=1)
    obs_blocks = obs_pert.reshape(OBLK, OBSB, M)
    innov_blocks = weighted_innovation.reshape(OBLK, OBSB)

    def block_impact(index):
        column = index // (REGIONS * BLK_DEV)
        sources = ((column + jnp.arange(3, dtype=jnp.int32) - 1) % CBLK).astype(jnp.int32)
        source_weights = weights[sources, index]
        source_sums = contracted[sources]
        combined = jnp.einsum('s,skt->kt', source_weights, source_sums, precision=lax.Precision.HIGHEST)
        result = jnp.dot(obs_blocks[index], combined, precision=lax.Precision.HIGHEST)
        return result * (innov_blocks[index] / (M - 1))[:, None]

    impact = lax.map(block_impact, jnp.arange(OBLK, dtype=jnp.int32))
    return impact.reshape(OBS, LEADS * T_SIZE)
```

```python
import functools

import jax
import jax.numpy as jnp
from jax import lax
from jax.experimental import pallas as pl
from jax.experimental.pallas import tpu as pltpu
from jax.sharding import PartitionSpec as P

M = 1024
OBSB = 128
MESH = pl.DeviceIdType.MESH


def extended(cells, sides, width):
    for axis, dim in sides:
        count = lax.axis_size(axis)
        head = lax.slice_in_dim(cells, 0, width, axis=dim)
        tail = lax.slice_in_dim(cells, cells.shape[dim] - width, cells.shape[dim], axis=dim)
        cells = jnp.concatenate(
            [
                lax.ppermute(tail, axis, [(i, (i + 1) % count) for i in range(count)]),
                cells,
                lax.ppermute(head, axis, [((i + 1) % count, i) for i in range(count)]),
            ],
            axis=dim,
        )
    return cells


def block_weights(
    obs_lists, block_taper, counts, column_index, region_index, owned_blocks, regions
):
    row_ids = lax.dynamic_index_in_dim(obs_lists, column_index, 0, keepdims=False)
    row_taper = lax.dynamic_index_in_dim(block_taper, column_index, 0, keepdims=False)
    row_count = lax.dynamic_index_in_dim(counts, column_index, 0, keepdims=False)
    slot_live = jnp.arange(row_ids.shape[0], dtype=jnp.int32) < row_count
    column_count = obs_lists.shape[0]
    owner_columns = (column_index + jnp.arange(3, dtype=jnp.int32) - 1) % column_count
    owner_ids = (owner_columns[:, None] * regions + region_index) * owned_blocks + jnp.arange(
        owned_blocks, dtype=jnp.int32
    )[None, :]
    matched = (owner_ids[:, :, None] == row_ids[None, None, :]) & slot_live[None, None, :]
    return jnp.sum(
        jnp.where(matched, row_taper[None, None, :], jnp.zeros((), row_taper.dtype)), axis=2
    )


def general_body(fcst_pert, sensitivity, obs_pert, weighted_innovation, obs_lists, block_taper, counts):
    regrouped = lax.all_to_all(fcst_pert, "mem", split_axis=3, concat_axis=1, tiled=True)
    leads = regrouped.shape[0]
    members = regrouped.shape[1]
    targets = sensitivity.shape[1]
    per_lead = []
    for lead in range(leads):
        left = regrouped[lead].reshape(members, -1)
        right = sensitivity[lead].reshape(targets, -1)
        per_lead.append(
            lax.dot_general(left, right, (((1,), (1,)), ((), ())), precision=lax.Precision.HIGHEST)
        )
    partial_sums = jnp.concatenate(per_lead, axis=1)
    summed = lax.psum(partial_sums, "dom")
    column_count = lax.axis_size("mem")
    regions = lax.axis_size("dom")
    column_index = lax.axis_index("mem")
    region_index = lax.axis_index("dom")
    owned_rows = obs_pert.shape[0]
    owned_blocks = owned_rows // OBSB
    row_scale = weighted_innovation / (M - 1)
    beside_all = extended(summed[None], (("mem", 0),), 1)
    source_rows = []
    for offset in (-1, 0, 1):
        source_column = (column_index + offset) % column_count
        weight_rows = block_weights(
            obs_lists, block_taper, counts, source_column, region_index, owned_blocks, regions
        )
        source_rows.append(weight_rows[1 - offset])
    source_weights = jnp.stack(source_rows, axis=0)
    combined = jnp.einsum(
        "sj,skt->jkt", source_weights, beside_all, precision=lax.Precision.HIGHEST
    )
    obs_blocks = obs_pert.reshape(owned_blocks, OBSB, members)
    result = jnp.einsum("jok,jkt->jot", obs_blocks, combined, precision=lax.Precision.HIGHEST)
    result = result.reshape(owned_rows, -1)
    return result * row_scale[:, None]


def halves(x):
    hi = x.astype(jnp.bfloat16)
    return hi, (x - hi.astype(jnp.float32)).astype(jnp.bfloat16)


def dot3(a, b, dims):
    d = functools.partial(
        lax.dot_general, dimension_numbers=(dims, ((), ())), preferred_element_type=jnp.float32
    )
    return d(a[0], b[0]) + d(a[0], b[1]) + d(a[1], b[0])


ORDER = ((0, 0), (1, 0), (0, 1), (2, 0), (1, 1), (3, 0), (2, 1), (3, 1))
LAG = 2


def kernel(
    f_hbm, s_hbm, o_hbm, wi_ref, lists_ref, taper_ref, counts_ref, out_ref,
    xf, obs, oh, ol, sg, pp, rs, cc, g, acc, scale,
    in_sem, a_send, a_recv, y_send, c_send, c_recv, d_send, d_recv, e_send, e_recv,
):
    m = lax.axis_index("mem")
    r = lax.axis_index("dom")
    z, y = m // 2, m % 2
    zx = (z, z + 1 - 2 * (z % 2), (z + 2) % 4, 3 - z)
    yx = (y, 1 - y)

    def block(j, i):
        return 2 * zx[j] + yx[i]

    rx = (r, r + 1 - 2 * (r % 2), (r + 2) % 4, 3 - r)

    cp_s = pltpu.make_async_copy(s_hbm, sg.at[m], in_sem.at[0])
    cp_f = pltpu.make_async_copy(f_hbm, xf, in_sem.at[1])
    cp_o = pltpu.make_async_copy(o_hbm, obs, in_sem.at[2])
    cp_s.start()
    cp_f.start()
    cp_o.start()

    barrier = pltpu.get_barrier_semaphore()
    for j, i in ORDER[1:]:
        pl.semaphore_signal(barrier, inc=1, device_id=(block(j, i), r), device_id_type=MESH)
    for k in (1, 2, 3):
        pl.semaphore_signal(barrier, inc=1, device_id=(m, rx[k]), device_id_type=MESH)
    cp_s.wait()
    pl.semaphore_wait(barrier, 10)

    def rcopy(src, dst, ss, rsem, dev):
        return pltpu.make_async_remote_copy(
            src_ref=src, dst_ref=dst, send_sem=ss, recv_sem=rsem, device_id=dev, device_id_type=MESH
        )

    def a_copy(j):
        return rcopy(sg.at[m], sg.at[m], a_send.at[j], a_recv.at[m], (block(j, 0), r))

    def a_arrival(b):
        return rcopy(sg.at[b], sg.at[b], a_send.at[0], a_recv.at[b], (block(0, 1), r))

    def y_copy(j):
        b = block(j, 0)
        return rcopy(sg.at[b], sg.at[b], y_send.at[j], a_recv.at[b], (block(0, 1), r))

    for j in (3, 2, 1):
        a_copy(j).start()
    y_copy(0).start()
    cp_f.wait()

    def c_copy(b, k):
        rows = pl.ds(pl.multiple_of(rx[k] * 32, 32), 32)
        return rcopy(
            pp.at[b, rows], rs.at[k - 1, b], c_send.at[k - 1, b], c_recv.at[k - 1, b], (m, rx[k])
        )

    def contract(j, i):
        b = block(j, i)
        if (j, i) != (0, 0):
            a_arrival(b).wait_recv()
        if i == 0 and j > 0:
            y_copy(j).start()
        for lead in range(2):
            left = xf[pl.ds(lead * 1024 + b, 128, stride=8), :]
            right = sg[b, lead * 64:(lead + 1) * 64, :]
            part = dot3(halves(left), halves(right), ((1,), (1,)))
            pp[b, :, lead * 64:(lead + 1) * 64] = part
        for k in (2, 3, 1):
            c_copy(b, k).start()

    def d_copy(b, s, q):
        return rcopy(cc.at[b], g.at[s, m, r], d_send.at[s, b], d_recv.at[s, m], (q, r))

    def finish(j, i):
        b = block(j, i)
        for k in (1, 2, 3):
            c_copy(b, k).wait_recv()
        own = pl.ds(pl.multiple_of(r * 32, 32), 32)
        total = (pp[b, own, :] + rs[0, b]) + (rs[1, b] + rs[2, b])
        cc[b] = total
        for s in range(3):
            q = (b + 9 - s) % 8

            @pl.when(q != m)
            def _():
                d_copy(b, s, q).start()

            @pl.when(q == m)
            def _():
                g[s, m, r] = total

    def prepare():
        cp_o.wait()

        @pl.loop(0, 6)
        def _(n):
            rows = pl.ds(pl.multiple_of(n * 128, 128), 128)
            hi, lo = halves(obs[rows, :])
            oh[rows, :] = hi
            ol[rows, :] = lo

        for n in range(6):
            col = jnp.broadcast_to(wi_ref[n:n + 1, :], (128, 128)).T * (1.0 / (M - 1))
            for s in range(3):
                source = (m + 7 + s) % 8
                ids = lists_ref[pl.ds(source, 1), :]
                tap = taper_ref[pl.ds(source, 1), :]
                live = lax.broadcasted_iota(jnp.int32, ids.shape, 1) < counts_ref[source]
                hit = (ids == (m * 4 + r) * 6 + n) & live
                w = jnp.sum(jnp.where(hit, tap, 0.0), axis=1, keepdims=True)
                scale[s, n] = col * w

    for n in range(8 + LAG):
        if n < 8:
            contract(*ORDER[n])
        if n == 0:
            prepare()
        if n >= LAG:
            finish(*ORDER[n - LAG])

    def e_copy(kind, src_m):
        if kind < 2:
            ref = g.at[:, src_m, r]
            to = rx[1 + kind]
        else:
            ref = g.at[:, src_m, rx[2]]
            to = rx[1]
        return rcopy(ref, ref, e_send.at[kind, src_m], e_recv.at[kind, src_m], (m, to))

    def e_arrival(kind, src_m):
        ref = g.at[:, src_m, rx[1 + kind]]
        return rcopy(ref, ref, e_send.at[kind, src_m], e_recv.at[kind, src_m], (m, rx[1]))

    def spread(j, i):
        b = block(j, i)
        if (j, i) != (0, 0):
            for s in range(3):
                rcopy(
                    cc.at[0], g.at[s, b, r], d_send.at[s, 0], d_recv.at[s, b], (b, r)
                ).wait_recv()
        e_copy(1, b).start()
        e_copy(0, b).start()

    def forward(j, i):
        b = block(j, i)
        e_arrival(1, b).wait_recv()
        e_copy(2, b).start()

    def multiply(j):
        for i in range(2):
            e_arrival(0, block(j, i)).wait_recv()
            e_arrival(2, block(j, i)).wait_recv()
        z0 = zx[j]
        both = jnp.concatenate(
            [g[s, pl.ds(2 * z0, 2)].reshape(256, 128) for s in range(3)], axis=1
        )
        chunk = halves(both)
        cols = pl.ds(pl.multiple_of(z0 * 256, 256), 256)
        for n in range(6):
            rows = slice(n * 128, (n + 1) * 128)
            part = dot3((oh[rows, cols], ol[rows, cols]), chunk, ((1,), (0,)))
            if j == 0:
                acc[rows, :] = part
            elif j < 3:
                acc[rows, :] = acc[rows, :] + part
            else:
                part = acc[rows, :] + part
                out_ref[rows, :] = (
                    scale[0, n] * part[:, 0:128]
                    + scale[1, n] * part[:, 128:256]
                    + scale[2, n] * part[:, 256:384]
                )

    flat = tuple((j, i) for j in range(4) for i in range(2))
    for n in range(8):
        spread(*flat[n])
        if n >= 1:
            forward(*flat[n - 1])
        if n >= 3 and n % 2 == 1:
            multiply((n - 3) // 2)
    forward(*flat[7])
    multiply(3)

    for j in (1, 2, 3):
        a_copy(j).wait_send()
    for j in range(4):
        y_copy(j).wait_send()
    for b in range(8):
        for k in (1, 2, 3):
            c_copy(b, k).wait_send()
        for s in range(3):
            q = (b + 9 - s) % 8

            @pl.when(q != m)
            def _():
                d_copy(b, s, q).wait_send()

        for kind in range(3):
            e_copy(kind, b).wait_send()


def body(fcst_pert, sensitivity, obs_pert, weighted_innovation, obs_lists, block_taper, counts):
    f = fcst_pert.reshape(2 * 128 * 8, 128)
    s = sensitivity.reshape(128, 128)
    wi = weighted_innovation.reshape(6, 128)
    any_spec = pl.BlockSpec(memory_space=pl.ANY)
    vmem = pl.BlockSpec(memory_space=pltpu.VMEM)
    f32, bf16, dma = jnp.float32, jnp.bfloat16, pltpu.SemaphoreType.DMA
    return pl.pallas_call(
        kernel,
        out_shape=jax.ShapeDtypeStruct((768, 128), f32),
        in_specs=[any_spec] * 3 + [vmem] * 3 + [pl.BlockSpec(memory_space=pltpu.SMEM)],
        out_specs=vmem,
        scratch_shapes=[
            pltpu.VMEM((2048, 128), f32),
            pltpu.VMEM((768, 1024), f32),
            pltpu.VMEM((768, 1024), bf16),
            pltpu.VMEM((768, 1024), bf16),
            pltpu.VMEM((8, 128, 128), f32),
            pltpu.VMEM((8, 128, 128), f32),
            pltpu.VMEM((3, 8, 32, 128), f32),
            pltpu.VMEM((8, 32, 128), f32),
            pltpu.VMEM((3, 8, 4, 32, 128), f32),
            pltpu.VMEM((768, 384), f32),
            pltpu.VMEM((3, 6, 128, 128), f32),
            dma((3,)), dma((4,)), dma((8,)), dma((4,)),
            dma((3, 8)), dma((3, 8)), dma((3, 8)), dma((3, 8)), dma((3, 8)), dma((3, 8)),
        ],
        compiler_params=pltpu.CompilerParams(
            collective_id=0, has_side_effects=True, vmem_limit_bytes=40 * 1024 * 1024
        ),
    )(f, s, obs_pert, wi, obs_lists, block_taper, counts)


def solution(mesh):
    in_specs = (
        P(None, "mem", "dom", None),
        P(None, None, "dom", "mem"),
        P(("mem", "dom"), None),
        P(("mem", "dom")),
        P(),
        P(),
        P(),
    )
    out_specs = P(("mem", "dom"), None)
    small = mesh.shape["mem"] == 8 and mesh.shape["dom"] == 4
    return jax.shard_map(
        body if small else general_body,
        mesh=mesh, in_specs=in_specs, out_specs=out_specs, check_vma=False,
    )
```

```python
import functools

import jax
import jax.numpy as jnp
from jax import lax
from jax.experimental import pallas as pl
from jax.experimental.pallas import tpu as pltpu
from jax.sharding import PartitionSpec as P

M = 1024
OBSB = 128
MESH = pl.DeviceIdType.MESH


def extended(cells, sides, width):
    for axis, dim in sides:
        count = lax.axis_size(axis)
        head = lax.slice_in_dim(cells, 0, width, axis=dim)
        tail = lax.slice_in_dim(cells, cells.shape[dim] - width, cells.shape[dim], axis=dim)
        cells = jnp.concatenate(
            [
                lax.ppermute(tail, axis, [(i, (i + 1) % count) for i in range(count)]),
                cells,
                lax.ppermute(head, axis, [((i + 1) % count, i) for i in range(count)]),
            ],
            axis=dim,
        )
    return cells


def block_weights(
    obs_lists, block_taper, counts, column_index, region_index, owned_blocks, regions
):
    row_ids = lax.dynamic_index_in_dim(obs_lists, column_index, 0, keepdims=False)
    row_taper = lax.dynamic_index_in_dim(block_taper, column_index, 0, keepdims=False)
    row_count = lax.dynamic_index_in_dim(counts, column_index, 0, keepdims=False)
    slot_live = jnp.arange(row_ids.shape[0], dtype=jnp.int32) < row_count
    column_count = obs_lists.shape[0]
    owner_columns = (column_index + jnp.arange(3, dtype=jnp.int32) - 1) % column_count
    owner_ids = (owner_columns[:, None] * regions + region_index) * owned_blocks + jnp.arange(
        owned_blocks, dtype=jnp.int32
    )[None, :]
    matched = (owner_ids[:, :, None] == row_ids[None, None, :]) & slot_live[None, None, :]
    return jnp.sum(
        jnp.where(matched, row_taper[None, None, :], jnp.zeros((), row_taper.dtype)), axis=2
    )


def general_body(fcst_pert, sensitivity, obs_pert, weighted_innovation, obs_lists, block_taper, counts):
    regrouped = lax.all_to_all(fcst_pert, "mem", split_axis=3, concat_axis=1, tiled=True)
    leads = regrouped.shape[0]
    members = regrouped.shape[1]
    targets = sensitivity.shape[1]
    per_lead = []
    for lead in range(leads):
        left = regrouped[lead].reshape(members, -1)
        right = sensitivity[lead].reshape(targets, -1)
        per_lead.append(
            lax.dot_general(left, right, (((1,), (1,)), ((), ())), precision=lax.Precision.HIGHEST)
        )
    partial_sums = jnp.concatenate(per_lead, axis=1)
    summed = lax.psum(partial_sums, "dom")
    column_count = lax.axis_size("mem")
    regions = lax.axis_size("dom")
    column_index = lax.axis_index("mem")
    region_index = lax.axis_index("dom")
    owned_rows = obs_pert.shape[0]
    owned_blocks = owned_rows // OBSB
    row_scale = weighted_innovation / (M - 1)
    beside_all = extended(summed[None], (("mem", 0),), 1)
    source_rows = []
    for offset in (-1, 0, 1):
        source_column = (column_index + offset) % column_count
        weight_rows = block_weights(
            obs_lists, block_taper, counts, source_column, region_index, owned_blocks, regions
        )
        source_rows.append(weight_rows[1 - offset])
    source_weights = jnp.stack(source_rows, axis=0)
    combined = jnp.einsum(
        "sj,skt->jkt", source_weights, beside_all, precision=lax.Precision.HIGHEST
    )
    obs_blocks = obs_pert.reshape(owned_blocks, OBSB, members)
    result = jnp.einsum("jok,jkt->jot", obs_blocks, combined, precision=lax.Precision.HIGHEST)
    result = result.reshape(owned_rows, -1)
    return result * row_scale[:, None]


def halves(x):
    hi = x.astype(jnp.bfloat16)
    return hi, (x - hi.astype(jnp.float32)).astype(jnp.bfloat16)


def dot3(a, b, dims):
    d = functools.partial(
        lax.dot_general, dimension_numbers=(dims, ((), ())), preferred_element_type=jnp.float32
    )
    return d(a[0], b[0]) + d(a[0], b[1]) + d(a[1], b[0])


ORDER = ((0, 0), (0, 1), (1, 0), (3, 0), (1, 1), (3, 1), (2, 0), (2, 1))
CHUNKS = (
    tuple((0, i, u) for u in (0, 1) for i in (0, 1))
    + tuple((j, i, u) for j in (1, 3) for i in (0, 1) for u in (0, 1))
    + tuple((j, i, 2) for j in (0, 1, 3) for i in (0, 1))
    + tuple((2, i, u) for i in (0, 1) for u in (0, 1, 2))
)
AT = (0, 0, 0, 0, 0, 0, 0, 4, 4, 4)
DONE = {0: 13, 1: 15, 3: 17, 2: 23}
PASS_LAG = 8


def kernel(
    f_hbm, s_hbm, o_hbm, wi_hbm, lists_hbm, taper_hbm, counts_hbm, out_ref,
    wi_ref, lists_ref, taper_ref, counts_ref, xf, obs, oh, ol, sg, pp, rs1, cx, rs2, cc, g, acc, scale,
    in_sem, a_send, a_recv, y_send, h_send, h_recv, c_send, c_recv, d_send, d_recv, e_send, e_recv,
):
    m = lax.axis_index("mem")
    r = lax.axis_index("dom")
    z, y = m // 2, m % 2
    x, c = r // 2, r % 2
    zx = (z, z + 1 - 2 * (z % 2), (z + 2) % 4, 3 - z)
    yx = (y, 1 - y)

    def block(j, i):
        return 2 * zx[j] + yx[i]

    rx = (r, r + 1 - 2 * (r % 2), (r + 2) % 4, 3 - r)

    cp_s = pltpu.make_async_copy(s_hbm, sg.at[m], in_sem.at[0])
    cp_f = pltpu.make_async_copy(f_hbm, xf, in_sem.at[1])
    cp_o = pltpu.make_async_copy(o_hbm, obs, in_sem.at[2])
    cp_s.start()
    cp_f.start()
    cp_o.start()
    cp_small = [
        pltpu.make_async_copy(src, dst, in_sem.at[3 + n])
        for n, (src, dst) in enumerate(
            ((wi_hbm, wi_ref), (lists_hbm, lists_ref), (taper_hbm, taper_ref), (counts_hbm, counts_ref))
        )
    ]
    for cp in cp_small:
        cp.start()

    barrier = pltpu.get_barrier_semaphore()
    for j, i in ORDER[1:]:
        pl.semaphore_signal(barrier, inc=1, device_id=(block(j, i), r), device_id_type=MESH)
    for k in (1, 2, 3):
        pl.semaphore_signal(barrier, inc=1, device_id=(m, rx[k]), device_id_type=MESH)
    cp_s.wait()
    pl.semaphore_wait(barrier, 10)

    def rcopy(src, dst, ss, rsem, dev):
        return pltpu.make_async_remote_copy(
            src_ref=src, dst_ref=dst, send_sem=ss, recv_sem=rsem, device_id=dev, device_id_type=MESH
        )

    def a_copy(j):
        return rcopy(sg.at[m], sg.at[m], a_send.at[j], a_recv.at[m], (block(j, 0), r))

    def a_arrival(b):
        return rcopy(sg.at[b], sg.at[b], a_send.at[0], a_recv.at[b], (block(0, 1), r))

    def y_copy(j):
        b = block(j, 0)
        return rcopy(sg.at[b], sg.at[b], y_send.at[j], a_recv.at[b], (block(0, 1), r))

    y_copy(0).start()
    for j in (1, 3, 2):
        a_copy(j).start()
    cp_f.wait()

    def h_copy(b):
        return rcopy(pp.at[b, 1 - c], rs1.at[b], h_send.at[b], h_recv.at[b], (m, rx[1]))

    def c_copy(b):
        return rcopy(cx.at[b], rs2.at[b], c_send.at[b], c_recv.at[b], (m, rx[2]))

    def contract(j, i):
        b = block(j, i)
        if (j, i) != (0, 0):
            a_arrival(b).wait_recv()
        if i == 0 and j > 0:
            y_copy(j).start()
        for lead in range(2):
            left = xf[pl.ds(lead * 1024 + b, 128, stride=8), :]
            right = sg[b, lead * 64:(lead + 1) * 64, :]
            part = dot3(halves(left), halves(right), ((1,), (1,)))
            for n in range(4):
                pp[b, n % 2, n // 2, :, lead * 64:(lead + 1) * 64] = part[n * 32:(n + 1) * 32]
        h_copy(b).start()

    def over_cores(j, i):
        b = block(j, i)
        h_copy(b).wait_recv()
        cx[b] = pp[b, c, 1 - x] + rs1[b, 1 - x]
        c_copy(b).start()
        cc[b] = pp[b, c, x] + rs1[b, x]

    def d_copy(b, s, q):
        return rcopy(cc.at[b], g.at[s, m, r], d_send.at[s, b], d_recv.at[s, m], (q, r))

    def finish(j, i):
        b = block(j, i)
        c_copy(b).wait_recv()
        total = cc[b] + rs2[b]
        cc[b] = total
        for s in range(3):
            q = (b + 9 - s) % 8

            @pl.when(q != m)
            def _():
                d_copy(b, s, q).start()

            @pl.when(q == m)
            def _():
                g[s, m, r] = total

    def prepare():
        cp_o.wait()
        for cp in cp_small:
            cp.wait()

        @pl.loop(0, 6)
        def _(n):
            rows = pl.ds(pl.multiple_of(n * 128, 128), 128)
            hi, lo = halves(obs[rows, :])
            oh[rows, :] = hi
            ol[rows, :] = lo

        for n in range(6):
            col = jnp.broadcast_to(wi_ref[n:n + 1, :], (128, 128)).T * (1.0 / (M - 1))
            for s in range(3):
                source = (m + 7 + s) % 8
                ids = lists_ref[pl.ds(source, 1), :]
                tap = taper_ref[pl.ds(source, 1), :]
                live = lax.broadcasted_iota(jnp.int32, ids.shape, 1) < counts_ref[source]
                hit = (ids == (m * 4 + r) * 6 + n) & live
                w = jnp.sum(jnp.where(hit, tap, 0.0), axis=1, keepdims=True)
                scale[s, n] = col * w

    def slot(u):
        return (1, 2 - 2 * y, 2 * y)[u]

    def e_copy(kind, src_m, s):
        if kind < 2:
            ref = g.at[s, src_m, r]
            to = rx[1 + kind]
        else:
            ref = g.at[s, src_m, rx[2]]
            to = rx[1]
        return rcopy(ref, ref, e_send.at[kind, src_m, s], e_recv.at[kind, src_m, s], (m, to))

    def e_arrival(kind, src_m, s):
        ref = g.at[s, src_m, rx[1 + kind]]
        return rcopy(ref, ref, e_send.at[kind, src_m, s], e_recv.at[kind, src_m, s], (m, rx[1]))

    def spread(j, i, u):
        b, s = block(j, i), slot(u)
        if (j, i) != (0, 0):
            rcopy(
                cc.at[0], g.at[s, b, r], d_send.at[s, 0], d_recv.at[s, b], (b, r)
            ).wait_recv()
        e_copy(1, b, s).start()
        e_copy(0, b, s).start()

    def forward(j, i, u):
        b, s = block(j, i), slot(u)
        e_arrival(1, b, s).wait_recv()
        e_copy(2, b, s).start()

    def multiply(j):
        for i in range(2):
            for s in range(3):
                e_arrival(0, block(j, i), s).wait_recv()
                e_arrival(2, block(j, i), s).wait_recv()
        z0 = zx[j]
        both = jnp.concatenate(
            [g[s, pl.ds(2 * z0, 2)].reshape(256, 128) for s in range(3)], axis=1
        )
        chunk = halves(both)
        cols = pl.ds(pl.multiple_of(z0 * 256, 256), 256)
        for n in range(6):
            rows = slice(n * 128, (n + 1) * 128)
            part = dot3((oh[rows, cols], ol[rows, cols]), chunk, ((1,), (0,)))
            if j == 0:
                acc[rows, :] = part
            elif j != 2:
                acc[rows, :] = acc[rows, :] + part
            else:
                part = acc[rows, :] + part
                out_ref[rows, :] = (
                    scale[0, n] * part[:, 0:128]
                    + scale[1, n] * part[:, 128:256]
                    + scale[2, n] * part[:, 256:384]
                )

    done = 0

    def passing(count):
        nonlocal done
        for n in range(done, done + count):
            if n < 24:
                spread(*CHUNKS[n])
            if PASS_LAG <= n < 24 + PASS_LAG:
                forward(*CHUNKS[n - PASS_LAG])
            for j in range(4):
                if n == DONE[j] + PASS_LAG + 1:
                    multiply(j)
        done += count

    for n in range(10):
        if n < 8:
            contract(*ORDER[n])
        if n == 0:
            prepare()
        if 1 <= n < 9:
            over_cores(*ORDER[n - 1])
        if n >= 2:
            finish(*ORDER[n - 2])
        passing(AT[n])
    passing(24 + PASS_LAG + 1 - done)

    for j in (1, 2, 3):
        a_copy(j).wait_send()
    for j in range(4):
        y_copy(j).wait_send()
    for b in range(8):
        h_copy(b).wait_send()
        c_copy(b).wait_send()
        for s in range(3):
            q = (b + 9 - s) % 8

            @pl.when(q != m)
            def _():
                d_copy(b, s, q).wait_send()

        for kind in range(3):
            for s in range(3):
                e_copy(kind, b, s).wait_send()


def body(fcst_pert, sensitivity, obs_pert, weighted_innovation, obs_lists, block_taper, counts):
    f = fcst_pert.reshape(2 * 128 * 8, 128)
    s = sensitivity.reshape(128, 128)
    wi = weighted_innovation.reshape(6, 128)
    any_spec = pl.BlockSpec(memory_space=pl.ANY)
    vmem = pl.BlockSpec(memory_space=pltpu.VMEM)
    f32, bf16, dma = jnp.float32, jnp.bfloat16, pltpu.SemaphoreType.DMA
    return pl.pallas_call(
        kernel,
        out_shape=jax.ShapeDtypeStruct((768, 128), f32),
        in_specs=[any_spec] * 7,
        out_specs=vmem,
        scratch_shapes=[
            pltpu.VMEM((6, 128), f32),
            pltpu.VMEM((8, 16), jnp.int32),
            pltpu.VMEM((8, 16), f32),
            pltpu.SMEM((8,), jnp.int32),
            pltpu.VMEM((2048, 128), f32),
            pltpu.VMEM((768, 1024), f32),
            pltpu.VMEM((768, 1024), bf16),
            pltpu.VMEM((768, 1024), bf16),
            pltpu.VMEM((8, 128, 128), f32),
            pltpu.VMEM((8, 2, 2, 32, 128), f32),
            pltpu.VMEM((8, 2, 32, 128), f32),
            pltpu.VMEM((8, 32, 128), f32),
            pltpu.VMEM((8, 32, 128), f32),
            pltpu.VMEM((8, 32, 128), f32),
            pltpu.VMEM((3, 8, 4, 32, 128), f32),
            pltpu.VMEM((768, 384), f32),
            pltpu.VMEM((3, 6, 128, 128), f32),
            dma((7,)), dma((4,)), dma((8,)), dma((4,)),
            dma((8,)), dma((8,)), dma((8,)), dma((8,)),
            dma((3, 8)), dma((3, 8)), dma((3, 8, 3)), dma((3, 8, 3)),
        ],
        compiler_params=pltpu.CompilerParams(
            collective_id=0, has_side_effects=True, vmem_limit_bytes=60 * 1024 * 1024
        ),
    )(f, s, obs_pert, wi, obs_lists, block_taper, counts)


def solution(mesh):
    in_specs = (
        P(None, "mem", "dom", None),
        P(None, None, "dom", "mem"),
        P(("mem", "dom"), None),
        P(("mem", "dom")),
        P(),
        P(),
        P(),
    )
    out_specs = P(("mem", "dom"), None)
    small = mesh.shape["mem"] == 8 and mesh.shape["dom"] == 4
    return jax.shard_map(
        body if small else general_body,
        mesh=mesh, in_specs=in_specs, out_specs=out_specs, check_vma=False,
    )
```

```python
import functools

import jax
import jax.numpy as jnp
from jax import lax
from jax.experimental import pallas as pl
from jax.experimental.pallas import tpu as pltpu
from jax.sharding import PartitionSpec as P

M = 1024
OBSB = 128
MESH = pl.DeviceIdType.MESH


def extended(cells, sides, width):
    for axis, dim in sides:
        count = lax.axis_size(axis)
        head = lax.slice_in_dim(cells, 0, width, axis=dim)
        tail = lax.slice_in_dim(cells, cells.shape[dim] - width, cells.shape[dim], axis=dim)
        cells = jnp.concatenate(
            [
                lax.ppermute(tail, axis, [(i, (i + 1) % count) for i in range(count)]),
                cells,
                lax.ppermute(head, axis, [((i + 1) % count, i) for i in range(count)]),
            ],
            axis=dim,
        )
    return cells


def block_weights(
    obs_lists, block_taper, counts, column_index, region_index, owned_blocks, regions
):
    row_ids = lax.dynamic_index_in_dim(obs_lists, column_index, 0, keepdims=False)
    row_taper = lax.dynamic_index_in_dim(block_taper, column_index, 0, keepdims=False)
    row_count = lax.dynamic_index_in_dim(counts, column_index, 0, keepdims=False)
    slot_live = jnp.arange(row_ids.shape[0], dtype=jnp.int32) < row_count
    column_count = obs_lists.shape[0]
    owner_columns = (column_index + jnp.arange(3, dtype=jnp.int32) - 1) % column_count
    owner_ids = (owner_columns[:, None] * regions + region_index) * owned_blocks + jnp.arange(
        owned_blocks, dtype=jnp.int32
    )[None, :]
    matched = (owner_ids[:, :, None] == row_ids[None, None, :]) & slot_live[None, None, :]
    return jnp.sum(
        jnp.where(matched, row_taper[None, None, :], jnp.zeros((), row_taper.dtype)), axis=2
    )


def general_body(fcst_pert, sensitivity, obs_pert, weighted_innovation, obs_lists, block_taper, counts):
    regrouped = lax.all_to_all(fcst_pert, "mem", split_axis=3, concat_axis=1, tiled=True)
    leads = regrouped.shape[0]
    members = regrouped.shape[1]
    targets = sensitivity.shape[1]
    per_lead = []
    for lead in range(leads):
        left = regrouped[lead].reshape(members, -1)
        right = sensitivity[lead].reshape(targets, -1)
        per_lead.append(
            lax.dot_general(left, right, (((1,), (1,)), ((), ())), precision=lax.Precision.HIGHEST)
        )
    partial_sums = jnp.concatenate(per_lead, axis=1)
    summed = lax.psum(partial_sums, "dom")
    column_count = lax.axis_size("mem")
    regions = lax.axis_size("dom")
    column_index = lax.axis_index("mem")
    region_index = lax.axis_index("dom")
    owned_rows = obs_pert.shape[0]
    owned_blocks = owned_rows // OBSB
    row_scale = weighted_innovation / (M - 1)
    beside_all = extended(summed[None], (("mem", 0),), 1)
    source_rows = []
    for offset in (-1, 0, 1):
        source_column = (column_index + offset) % column_count
        weight_rows = block_weights(
            obs_lists, block_taper, counts, source_column, region_index, owned_blocks, regions
        )
        source_rows.append(weight_rows[1 - offset])
    source_weights = jnp.stack(source_rows, axis=0)
    combined = jnp.einsum(
        "sj,skt->jkt", source_weights, beside_all, precision=lax.Precision.HIGHEST
    )
    obs_blocks = obs_pert.reshape(owned_blocks, OBSB, members)
    result = jnp.einsum("jok,jkt->jot", obs_blocks, combined, precision=lax.Precision.HIGHEST)
    result = result.reshape(owned_rows, -1)
    return result * row_scale[:, None]


def halves(x):
    hi = x.astype(jnp.bfloat16)
    return hi, (x - hi.astype(jnp.float32)).astype(jnp.bfloat16)


def dot3(a, b, dims):
    d = functools.partial(
        lax.dot_general, dimension_numbers=(dims, ((), ())), preferred_element_type=jnp.float32
    )
    return d(a[0], b[0]) + d(a[0], b[1]) + d(a[1], b[0])


ORDER = ((0, 0), (0, 1), (1, 0), (3, 0), (1, 1), (3, 1), (2, 0), (2, 1))
CHUNKS = (
    tuple((0, i, u) for u in (0, 1) for i in (0, 1))
    + tuple((j, i, u) for j in (1, 3) for i in (0, 1) for u in (0, 1))
    + tuple((j, i, 2) for j in (0, 1, 3) for i in (0, 1))
    + tuple((2, i, u) for i in (0, 1) for u in (0, 1, 2))
)
AT = (0, 0, 0, 0, 0, 0, 0, 0, 4, 4, 4)
DONE = {0: 13, 1: 15, 3: 17, 2: 23}
PASS_LAG = 8


def kernel(
    f_hbm, s_hbm, o_hbm, wi_hbm, lists_hbm, taper_hbm, counts_hbm, out_ref,
    wi_ref, lists_ref, taper_ref, counts_ref, xf, obs, oh, ol, sg, pp, rs1, cx, rs2, cc, g, acc, scale,
    in_sem, a_send, a_recv, y_send, h_send, h_recv, c_send, c_recv, d_send, d_recv, e_send, e_recv,
):
    m = lax.axis_index("mem")
    r = lax.axis_index("dom")
    z, y = m // 2, m % 2
    x, c = r // 2, r % 2
    zx = (z, z + 1 - 2 * (z % 2), (z + 2) % 4, 3 - z)
    yx = (y, 1 - y)

    def block(j, i):
        return 2 * zx[j] + yx[i]

    rx = (r, r + 1 - 2 * (r % 2), (r + 2) % 4, 3 - r)

    cp_s = pltpu.make_async_copy(s_hbm, sg.at[m], in_sem.at[0])
    cp_f = pltpu.make_async_copy(f_hbm, xf, in_sem.at[1])
    cp_o = pltpu.make_async_copy(o_hbm, obs, in_sem.at[2])
    cp_s.start()
    cp_f.start()
    cp_o.start()
    cp_small = [
        pltpu.make_async_copy(src, dst, in_sem.at[3 + n])
        for n, (src, dst) in enumerate(
            ((wi_hbm, wi_ref), (lists_hbm, lists_ref), (taper_hbm, taper_ref), (counts_hbm, counts_ref))
        )
    ]
    for cp in cp_small:
        cp.start()

    barrier = pltpu.get_barrier_semaphore()
    for j, i in ORDER[1:]:
        pl.semaphore_signal(barrier, inc=1, device_id=(block(j, i), r), device_id_type=MESH)
    for k in (1, 2, 3):
        pl.semaphore_signal(barrier, inc=1, device_id=(m, rx[k]), device_id_type=MESH)
    cp_s.wait()
    pl.semaphore_wait(barrier, 10)

    def rcopy(src, dst, ss, rsem, dev):
        return pltpu.make_async_remote_copy(
            src_ref=src, dst_ref=dst, send_sem=ss, recv_sem=rsem, device_id=dev, device_id_type=MESH
        )

    def a_copy(j):
        return rcopy(sg.at[m], sg.at[m], a_send.at[j], a_recv.at[m], (block(j, 0), r))

    def a_arrival(b):
        return rcopy(sg.at[b], sg.at[b], a_send.at[0], a_recv.at[b], (block(0, 1), r))

    def y_copy(j):
        b = block(j, 0)
        return rcopy(sg.at[b], sg.at[b], y_send.at[j], a_recv.at[b], (block(0, 1), r))

    y_copy(0).start()
    for j in (1, 3, 2):
        a_copy(j).start()
    cp_f.wait()

    def h_copy(b):
        return rcopy(pp.at[b, 1 - c], rs1.at[b], h_send.at[b], h_recv.at[b], (m, rx[1]))

    def c_copy(b):
        return rcopy(cx.at[b], rs2.at[b], c_send.at[b], c_recv.at[b], (m, rx[2]))

    def contract(j, i):
        b = block(j, i)
        if (j, i) != (0, 0):
            a_arrival(b).wait_recv()
        if i == 0 and j > 0:
            y_copy(j).start()
        for lead in range(2):
            left = xf[pl.ds(lead * 1024 + b, 128, stride=8), :]
            right = sg[b, lead * 64:(lead + 1) * 64, :]
            part = dot3(halves(left), halves(right), ((1,), (1,)))
            for n in range(4):
                pp[b, n % 2, n // 2, :, lead * 64:(lead + 1) * 64] = part[n * 32:(n + 1) * 32]
        h_copy(b).start()

    def over_cores(j, i):
        b = block(j, i)
        h_copy(b).wait_recv()
        cx[b] = pp[b, c, 1 - x] + rs1[b, 1 - x]
        c_copy(b).start()
        cc[b] = pp[b, c, x] + rs1[b, x]

    def d_copy(b, s, q):
        return rcopy(cc.at[b], g.at[s, m, r], d_send.at[s, b], d_recv.at[s, m], (q, r))

    def finish(j, i):
        b = block(j, i)
        c_copy(b).wait_recv()
        total = cc[b] + rs2[b]
        cc[b] = total
        for s in range(3):
            q = (b + 9 - s) % 8

            @pl.when(q != m)
            def _():
                d_copy(b, s, q).start()

            @pl.when(q == m)
            def _():
                g[s, m, r] = total

    def prepare():
        cp_o.wait()
        for cp in cp_small:
            cp.wait()

        @pl.loop(0, 6)
        def _(n):
            rows = pl.ds(pl.multiple_of(n * 128, 128), 128)
            hi, lo = halves(obs[rows, :])
            oh[rows, :] = hi
            ol[rows, :] = lo

        for n in range(6):
            col = jnp.broadcast_to(wi_ref[n:n + 1, :], (128, 128)).T * (1.0 / (M - 1))
            for s in range(3):
                source = (m + 7 + s) % 8
                ids = lists_ref[pl.ds(source, 1), :]
                tap = taper_ref[pl.ds(source, 1), :]
                live = lax.broadcasted_iota(jnp.int32, ids.shape, 1) < counts_ref[source]
                hit = (ids == (m * 4 + r) * 6 + n) & live
                w = jnp.sum(jnp.where(hit, tap, 0.0), axis=1, keepdims=True)
                scale[s, n] = col * w

    def slot(u):
        return (1, 2 - 2 * y, 2 * y)[u]

    def e_copy(kind, src_m, s):
        if kind < 2:
            ref = g.at[s, src_m, r]
            to = rx[1 + kind]
        else:
            ref = g.at[s, src_m, rx[2]]
            to = rx[1]
        return rcopy(ref, ref, e_send.at[kind, src_m, s], e_recv.at[kind, src_m, s], (m, to))

    def e_arrival(kind, src_m, s):
        ref = g.at[s, src_m, rx[1 + kind]]
        return rcopy(ref, ref, e_send.at[kind, src_m, s], e_recv.at[kind, src_m, s], (m, rx[1]))

    def spread(j, i, u):
        b, s = block(j, i), slot(u)
        if (j, i) != (0, 0):
            rcopy(
                cc.at[0], g.at[s, b, r], d_send.at[s, 0], d_recv.at[s, b], (b, r)
            ).wait_recv()
        e_copy(1, b, s).start()
        e_copy(0, b, s).start()

    def forward(j, i, u):
        b, s = block(j, i), slot(u)
        e_arrival(1, b, s).wait_recv()
        e_copy(2, b, s).start()

    def multiply(j):
        for i in range(2):
            for s in range(3):
                e_arrival(0, block(j, i), s).wait_recv()
                e_arrival(2, block(j, i), s).wait_recv()
        z0 = zx[j]
        both = jnp.concatenate(
            [g[s, pl.ds(2 * z0, 2)].reshape(256, 128) for s in range(3)], axis=1
        )
        chunk = halves(both)
        cols = pl.ds(pl.multiple_of(z0 * 256, 256), 256)
        for n in range(6):
            rows = slice(n * 128, (n + 1) * 128)
            part = dot3((oh[rows, cols], ol[rows, cols]), chunk, ((1,), (0,)))
            if j == 0:
                acc[rows, :] = part
            elif j != 2:
                acc[rows, :] = acc[rows, :] + part
            else:
                part = acc[rows, :] + part
                out_ref[rows, :] = (
                    scale[0, n] * part[:, 0:128]
                    + scale[1, n] * part[:, 128:256]
                    + scale[2, n] * part[:, 256:384]
                )

    done = 0

    def passing(count):
        nonlocal done
        for n in range(done, done + count):
            if n < 24:
                spread(*CHUNKS[n])
            if PASS_LAG <= n < 24 + PASS_LAG:
                forward(*CHUNKS[n - PASS_LAG])
            for j in range(4):
                if n == DONE[j] + PASS_LAG + 1:
                    multiply(j)
        done += count

    for n in range(11):
        if n < 8:
            contract(*ORDER[n])
        if n == 0:
            prepare()
        if 1 <= n < 9:
            over_cores(*ORDER[n - 1])
        if n >= 3:
            finish(*ORDER[n - 3])
        passing(AT[n])
    passing(24 + PASS_LAG + 1 - done)

    for j in (1, 2, 3):
        a_copy(j).wait_send()
    for j in range(4):
        y_copy(j).wait_send()
    for b in range(8):
        h_copy(b).wait_send()
        c_copy(b).wait_send()
        for s in range(3):
            q = (b + 9 - s) % 8

            @pl.when(q != m)
            def _():
                d_copy(b, s, q).wait_send()

        for kind in range(3):
            for s in range(3):
                e_copy(kind, b, s).wait_send()


def body(fcst_pert, sensitivity, obs_pert, weighted_innovation, obs_lists, block_taper, counts):
    f = fcst_pert.reshape(2 * 128 * 8, 128)
    s = sensitivity.reshape(128, 128)
    wi = weighted_innovation.reshape(6, 128)
    any_spec = pl.BlockSpec(memory_space=pl.ANY)
    vmem = pl.BlockSpec(memory_space=pltpu.VMEM)
    f32, bf16, dma = jnp.float32, jnp.bfloat16, pltpu.SemaphoreType.DMA
    return pl.pallas_call(
        kernel,
        out_shape=jax.ShapeDtypeStruct((768, 128), f32),
        in_specs=[any_spec] * 7,
        out_specs=vmem,
        scratch_shapes=[
            pltpu.VMEM((6, 128), f32),
            pltpu.VMEM((8, 16), jnp.int32),
            pltpu.VMEM((8, 16), f32),
            pltpu.SMEM((8,), jnp.int32),
            pltpu.VMEM((2048, 128), f32),
            pltpu.VMEM((768, 1024), f32),
            pltpu.VMEM((768, 1024), bf16),
            pltpu.VMEM((768, 1024), bf16),
            pltpu.VMEM((8, 128, 128), f32),
            pltpu.VMEM((8, 2, 2, 32, 128), f32),
            pltpu.VMEM((8, 2, 32, 128), f32),
            pltpu.VMEM((8, 32, 128), f32),
            pltpu.VMEM((8, 32, 128), f32),
            pltpu.VMEM((8, 32, 128), f32),
            pltpu.VMEM((3, 8, 4, 32, 128), f32),
            pltpu.VMEM((768, 384), f32),
            pltpu.VMEM((3, 6, 128, 128), f32),
            dma((7,)), dma((4,)), dma((8,)), dma((4,)),
            dma((8,)), dma((8,)), dma((8,)), dma((8,)),
            dma((3, 8)), dma((3, 8)), dma((3, 8, 3)), dma((3, 8, 3)),
        ],
        compiler_params=pltpu.CompilerParams(
            collective_id=0, has_side_effects=True, vmem_limit_bytes=60 * 1024 * 1024
        ),
    )(f, s, obs_pert, wi, obs_lists, block_taper, counts)


def solution(mesh):
    in_specs = (
        P(None, "mem", "dom", None),
        P(None, None, "dom", "mem"),
        P(("mem", "dom"), None),
        P(("mem", "dom")),
        P(),
        P(),
        P(),
    )
    out_specs = P(("mem", "dom"), None)
    small = mesh.shape["mem"] == 8 and mesh.shape["dom"] == 4
    return jax.shard_map(
        body if small else general_body,
        mesh=mesh, in_specs=in_specs, out_specs=out_specs, check_vma=False,
    )
```
